512 devices in a mesh: member: 8 (over y_hi, x), space: 64 (over z, y_lo, core).
Axes of the slice: x: 4, y: 4 (y_hi: 2, y_lo: 2; y = y_hi * 2 + y_lo), z: 16, core: 2. Of those that a mesh axis runs over, the one named last changes fastest.
Arguments:
- latent: bfloat16 [8, 4096, 1024], P('member', 'space'), may hold values from -6 to 6
- neighbours: int32 [4, 32768], P(None, 'space'), may hold values from 0 to 4095, as said below
- live: int32 [4, 32768], P(None, 'space'), may hold values 0 or 1
- edge_weight: bfloat16 [4, 32768], P(None, 'space'), may hold values from 0.19921875 to 1
- area: float32 [32768], P('space'), may hold values from 0.5 to 4
- targets: float32 [100, 32768], P(None, 'space'), may hold values from -5 to 5
- w_in: bfloat16 [1024, 1024], replicated, may hold values from -0.1875 to 0.1875
- w_out: bfloat16 [100, 1024], replicated, may hold values from -0.1875 to 0.1875
Outputs:
- grad_latent: bfloat16 [8, 4096, 1024], P('member', 'space')
The draws below stay inside these ranges and needn't reach their ends.
Inputs may be any that keep to these rules, and one draw needn't show every extreme that they name: `neighbours`: grid point g = s * 512 + j (space shard s) names in each slot a mesh node within 32 places, cyclically modulo 4096, of node s * 64 + floor(j * 64 / 512); the 4 slots of one grid point name distinct nodes; the first and last grid point of every shard reach the full distance 32 below and above.
All inputs are finite; a program needn't handle non-finite values. No bound on the sum of `live` on one device may be relied on, other than what follows from the above.
Results may differ from the reference program's by a relative error of at most 0.01.
Values may be sent and summed in bfloat16 or wider, within the bound.
No kernel may reach another device: no remote copies, remote signals or barrier semaphores. Data moves between devices by JAX's collectives and lax.ppermute only.
A program may use at most 64 MiB of HBM per device.

```python
import math
import jax
import jax.numpy as jnp
from jax import lax

C = 1024
F = 100
K = 4
HALO = 32
G_DEV = 512
NM_DEV = 64
M = 8
GRID = 32768
MESH = 4096


def draw_neighbours(key, part):
    key = jax.random.fold_in(key, 11)
    span = 2 * HALO + 1
    position = jnp.arange(GRID, dtype=jnp.int32)
    shard = position // G_DEV
    within = position % G_DEV
    centre = shard * NM_DEV + within * NM_DEV // G_DEV
    column = jnp.arange(span, dtype=jnp.int32)
    score = jax.random.randint(key, (GRID, span), 0, 1 << 20, dtype=jnp.int32) * 256 + column[None, :]
    score = jnp.where((within == 0)[:, None] & (column == 0)[None, :], -1, score)
    score = jnp.where((within == G_DEV - 1)[:, None] & (column == span - 1)[None, :], -1, score)
    order = jnp.argsort(score, axis=1)[:, :K].astype(jnp.int32)
    nodes = jnp.mod(centre[:, None] + order - HALO, MESH)
    return nodes.T.astype(jnp.int32)


def plant(result, key, smallest, largest):
    extent = result.shape
    place = [jax.random.randint(jax.random.fold_in(key, axis), (), 0, extent[axis]) for axis in range(len(extent))]
    result = result.at[tuple(place)].set(smallest)
    longest = extent.index(max(extent))
    place[longest] = (place[longest] + 1) % extent[longest]
    return result.at[tuple(place)].set(largest)


def levels(key, dims, shards, least, top_value):
    level, own = 1.0, jax.random.fold_in(key, 6)
    for dim, blocks in shards:
        heights = jnp.exp(jax.random.uniform(jax.random.fold_in(own, dim), (blocks,), jnp.float32, least / len(shards), top_value / len(shards)))
        level = level * jnp.repeat(heights, dims[dim] // blocks).reshape([-1 if axis == dim else 1 for axis in range(len(dims))])
    return level


def noise(rng, dims, spread, limit, pieces=(), kind=jnp.bfloat16):
    gain = levels(rng, dims, pieces, -0.22, 0.18) if pieces else 1.0
    result = jax.random.normal(rng, dims, jnp.float32) * spread * gain
    return jnp.minimum(jnp.maximum(result, -limit), limit).astype(kind)


def setup_inputs(seed: int = 0) -> dict:
    streams_of = jax.random.split(jax.random.key(seed), 9)
    return {
        "latent": noise(streams_of[0], (M, MESH, C), 1.0, 6.0, ((0, 8), (1, 64))),
        "neighbours": draw_neighbours(jax.random.fold_in(streams_of[8], 71), 0),
        "live": plant((jax.random.randint(streams_of[2], (K, GRID), 0, 4) < 3).astype(jnp.int32), jax.random.fold_in(streams_of[2], 1), 0, 1),
        "edge_weight": jnp.clip(0.19921875 + 0.80078125 * jax.random.uniform(streams_of[3], (K, GRID), jnp.float32) ** levels(streams_of[3], (K, GRID), ((1, 64),), -0.2, 0.2), 0.19921875, 1.0).astype(jnp.bfloat16),
        "area": jnp.clip(jnp.exp(math.log(4.0) - 2.0794415 * jax.random.uniform(streams_of[4], (GRID,), jnp.float32) ** levels(streams_of[4], (GRID,), ((0, 64),), -0.2, 0.2)), 0.5, 4.0),
        "targets": noise(streams_of[5], (F, GRID), 0.7, 5.0, ((1, 64),), jnp.float32),
        "w_in": noise(streams_of[6], (C, C), C ** -0.5, 0.1875),
        "w_out": noise(streams_of[7], (F, C), C ** -0.5, 0.1875),
    }


smooth = 0.0025

def slope(diff):
    return diff / jnp.sqrt(diff * diff + smooth)

def decode(member_latent, neighbours, coef, w_in, w_out):
    joined = jnp.zeros((neighbours.shape[1], member_latent.shape[1]), jnp.float32)
    for slot in range(K):
        joined = joined + coef[slot][:, None] * member_latent[neighbours[slot]].astype(jnp.float32)
    joined = joined.astype(jnp.bfloat16)
    pre = jnp.dot(joined, w_in, preferred_element_type=jnp.float32)
    hidden = jax.nn.silu(pre).astype(jnp.bfloat16)
    field = lax.dot_general(w_out, hidden, (((1,), (1,)), ((), ())), preferred_element_type=jnp.float32)
    return (field, pre)

def reference(latent, neighbours, live, edge_weight, area, targets, w_in, w_out):
    coef = edge_weight.astype(jnp.float32) * live.astype(jnp.float32)
    members = latent.shape[0]

    def forward_one(member_latent):
        return decode(member_latent, neighbours, coef, w_in, w_out)[0]
    fields = lax.map(forward_one, latent)
    pairwise = jnp.zeros_like(fields)
    for other in range(members):
        pairwise = pairwise + slope(fields - fields[other][None])
    grad_field = area[None, None, :] * (slope(fields - targets[None]) - pairwise / (members - 1))
    grad_field = grad_field.astype(jnp.bfloat16)

    def backward_one(pair):
        member_latent, member_grad = pair
        field, pre = decode(member_latent, neighbours, coef, w_in, w_out)
        grad_hidden = lax.dot_general(member_grad, w_out, (((0,), (0,)), ((), ())), preferred_element_type=jnp.float32)
        sig = jax.nn.sigmoid(pre)
        grad_pre = (grad_hidden * sig * (1.0 + pre * (1.0 - sig))).astype(jnp.bfloat16)
        grad_joined = lax.dot_general(grad_pre, w_in, (((1,), (1,)), ((), ())), preferred_element_type=jnp.float32)
        grad_joined = grad_joined.astype(jnp.bfloat16).astype(jnp.float32)
        total = jnp.zeros(member_latent.shape, jnp.float32)
        for slot in range(K):
            total = total.at[neighbours[slot]].add(coef[slot][:, None] * grad_joined)
        return total.astype(jnp.bfloat16)
    return lax.map(backward_one, (latent, grad_field))
```

```python
import jax
import jax.numpy as jnp
from jax import lax
from jax.sharding import PartitionSpec as P

HALO = 32


smooth = 0.0025


def extended_2(block, sides, width):
    for axis, dim in sides:
        count = lax.axis_size(axis)
        forward = [(i, i + 1) for i in range(count - 1)]
        forward.append((count - 1, 0))
        backward = [(target, source) for source, target in forward]
        low = lax.ppermute(
            lax.slice_in_dim(block, block.shape[dim] - width, None, axis=dim), axis, forward
        )
        high = lax.ppermute(lax.slice_in_dim(block, 0, width, axis=dim), axis, backward)
        block = jnp.concatenate([low, block, high], axis=dim)
    return block


def from_behind(shard, axis, by):
    size = lax.axis_size(axis)
    return lax.ppermute(shard, axis, [(i, (i + by) % size) for i in range(size)])


def slope(diff):
    return diff / jnp.sqrt(diff * diff + smooth)


def per_device(latent, neighbours, live, edge_weight, area, targets, w_in, w_out):
    rows = latent.shape[1]
    spaces = lax.axis_size("space")
    members = lax.axis_size("member") * latent.shape[0]
    offset = lax.axis_index("space") * rows - HALO
    extended = extended_2(latent[0], (("space", 0),), HALO)
    span_rows = rows + 2 * HALO
    local_rows = jnp.mod(neighbours - offset, rows * spaces)
    coef = edge_weight * live.astype(jnp.bfloat16)
    column = jnp.arange(span_rows, dtype=jnp.int32)
    picks = jnp.where(
        local_rows[:, :, None] == column[None, None, :],
        coef[:, :, None],
        jnp.zeros((), jnp.bfloat16),
    )
    adjacency = jnp.sum(picks, axis=0, dtype=jnp.bfloat16)
    joined = jnp.dot(adjacency, extended, preferred_element_type=jnp.float32).astype(jnp.bfloat16)
    pre = jnp.dot(joined, w_in, preferred_element_type=jnp.float32)
    hidden = jax.nn.silu(pre).astype(jnp.bfloat16)
    field = lax.dot_general(
        w_out, hidden, (((1,), (1,)), ((), ())), preferred_element_type=jnp.float32
    )
    own_term = slope(field - targets)
    copies = jnp.broadcast_to(field.astype(jnp.bfloat16)[None], (members,) + field.shape)
    every = lax.all_to_all(copies, "member", 0, 0, tiled=True)
    me = lax.axis_index("member")
    others = (jnp.arange(members) != me)[:, None, None]
    diffs = field[None] - every.astype(jnp.float32)
    pairwise = jnp.sum(jnp.where(others, slope(diffs), 0.0), axis=0)
    grad_field = (area[None, :] * (own_term - pairwise / (members - 1))).astype(jnp.bfloat16)
    grad_hidden = lax.dot_general(
        grad_field, w_out, (((0,), (0,)), ((), ())), preferred_element_type=jnp.float32
    )
    sigma = jax.nn.sigmoid(pre)
    grad_pre = (grad_hidden * sigma * (1.0 + pre * (1.0 - sigma))).astype(jnp.bfloat16)
    grad_joined = lax.dot_general(
        grad_pre, w_in, (((1,), (1,)), ((), ())), preferred_element_type=jnp.float32
    ).astype(jnp.bfloat16)
    grad_extended = lax.dot_general(
        adjacency, grad_joined, (((0,), (0,)), ((), ())), preferred_element_type=jnp.float32
    )
    upper_rim = grad_extended[:HALO]
    lower_rim = grad_extended[span_rows - HALO :]
    from_after = from_behind(upper_rim, "space", -1)
    from_before = from_behind(lower_rim, "space", 1)
    inner = grad_extended[HALO : HALO + rows]
    inner = inner.at[:HALO].add(from_before)
    inner = inner.at[rows - HALO :].add(from_after)
    return inner.astype(jnp.bfloat16)[None]


def solution(mesh):
    return jax.shard_map(
        per_device,
        mesh=mesh,
        in_specs=(
            P("member", "space", None),
            P(None, "space"),
            P(None, "space"),
            P(None, "space"),
            P("space"),
            P(None, "space"),
            P(),
            P(),
        ),
        out_specs=P("member", "space", None),
        check_vma=False,
    )
```

```python
import jax
import jax.numpy as jnp
from jax import lax
from jax.experimental import pallas as pl
from jax.experimental.pallas import tpu as pltpu
from jax.sharding import PartitionSpec as P

smooth = 0.0025
bf16 = jnp.bfloat16
f32 = jnp.float32
STEP = 256


def shifted(block, axis, by):
    size = lax.axis_size(axis)
    return lax.ppermute(block, axis, [(i, (i + by) % size) for i in range(size)])


def slope(diff):
    return diff * lax.rsqrt(diff * diff + smooth)


def product(left, right, over):
    return lax.dot_general(left, right, (over, ((), ())), preferred_element_type=f32)


def pack_kernel(mesh_rows, latent, neighbours, live, weight, message):
    rows, half = latent.shape[0], neighbours.shape[1] // 2
    message[:rows] = latent[...]
    first = lax.axis_index("space") * rows
    place = jnp.bitwise_and(neighbours[:, half:] - first, mesh_rows - 1).astype(f32)
    coef = weight[:, half:].astype(f32) * live[:, half:].astype(f32)
    slots = neighbours.shape[0]
    place = jnp.concatenate([place[k : k + 1] for k in range(slots)], axis=1)
    coef = jnp.concatenate([coef[k : k + 1] for k in range(slots)], axis=1)
    row = lax.broadcasted_iota(jnp.int32, (16, place.shape[1]), 0)
    message[rows:] = jnp.where(row == 0, place, jnp.where(row == 1, coef, 0.0)).astype(bf16)


def forward_kernel(
    mesh_rows, message, latent, neighbours, live, weight, w_in, w_out,
    copies, field, gate, adjacency, mixed, hidden,
):
    rows, half = latent.shape[0], neighbours.shape[1] // 2
    slots, channels = neighbours.shape[0], latent.shape[1]
    span = 2 * rows
    row = lax.broadcasted_iota(jnp.int32, (span, half), 0)
    tail = message[rows:].astype(f32)
    first = (lax.axis_index("space") - 1) * rows
    near = jnp.bitwise_and(neighbours[:, :half] - first, mesh_rows - 1)
    near_coef = weight[:, :half].astype(f32) * live[:, :half].astype(f32)
    low = jnp.zeros((span, half), f32)
    high = jnp.zeros((span, half), f32)
    for k in range(slots):
        cut = slice(k * half, (k + 1) * half)
        low = low + jnp.where(row == tail[0:1, cut].astype(jnp.int32), tail[1:2, cut], 0.0)
        high = high + jnp.where(row == near[k : k + 1], near_coef[k : k + 1], 0.0)
    adjacency[:, :half] = low.astype(bf16)
    adjacency[:, half:] = high.astype(bf16)
    edges = adjacency[...]
    twice = jnp.concatenate([edges, edges], axis=0)
    both = jnp.concatenate([message[:rows], latent[...]], axis=0)
    for c in range(0, channels, STEP):
        part = product(both, w_in[:, c : c + STEP], ((1,), (0,)))
        top = part.astype(bf16)
        mixed[:span, c : c + STEP] = top
        mixed[span:, c : c + STEP] = (part - top.astype(f32)).astype(bf16)
    for c in range(0, channels, STEP):
        pre = product(mixed[:, c : c + STEP], twice, ((0,), (0,)))
        sigma = 1.0 / (1.0 + jnp.exp(-pre))
        act = pre * sigma
        hidden[c : c + STEP] = act.astype(bf16)
        gate[c : c + STEP] = sigma + act * (1.0 - sigma)
    out = product(w_out[...], hidden[...], ((1,), (0,)))
    field[...] = out
    rounded = out.astype(bf16)
    for m in range(copies.shape[0]):
        copies[m] = rounded


def backward_kernel(
    every, field, targets, area, moved, gate, adjacency, w_out, w_in, out, rim, joined
):
    members, fields, points = every.shape
    half = points // 2
    rows = out.shape[0]
    me = lax.axis_index("member")
    own = field[...]
    total = jnp.zeros((fields, points), f32)
    for m in range(members):
        total = total + slope(own - every[m].astype(f32)) * jnp.where(me == m, 0.0, 1.0 / (members - 1))
    goal = jnp.concatenate([moved[:fields], targets[:, :half]], axis=1)
    scale = jnp.concatenate([moved[fields : fields + 1], area[:, :half]], axis=1)
    grad_field = (scale * (slope(own - goal) - total)).astype(bf16)
    edges = adjacency[...]
    for c in range(0, gate.shape[0], STEP):
        grad_hidden = product(w_out[:, c : c + STEP], grad_field, ((0,), (0,)))
        grad_pre = (grad_hidden * gate[c : c + STEP]).astype(bf16)
        joined[:, c : c + STEP] = product(edges, grad_pre, ((1,), (1,))).astype(bf16)
    for c in range(0, w_in.shape[0], STEP):
        part = product(joined[...], w_in[c : c + STEP], ((1,), (1,)))
        rim[:, c : c + STEP] = part[:rows].astype(bf16)
        out[:, c : c + STEP] = part[rows:]


def call(kernel, outs, scratch, *operands):
    vmem = pl.BlockSpec(memory_space=pltpu.VMEM)
    return pl.pallas_call(
        kernel,
        out_shape=outs,
        in_specs=[vmem] * len(operands),
        out_specs=[vmem] * len(outs),
        scratch_shapes=scratch,
        compiler_params=pltpu.CompilerParams(vmem_limit_bytes=40 << 20),
    )(*operands)


def per_device(latent, neighbours, live, edge_weight, area, targets, w_in, w_out):
    rows, channels = latent.shape[1:]
    points = neighbours.shape[1]
    fields = targets.shape[0]
    half = points // 2
    mesh_rows = rows * lax.axis_size("space")
    members = lax.axis_size("member")
    span = 2 * rows

    def shape(dims, kind):
        return jax.ShapeDtypeStruct(dims, kind)

    (message,) = call(
        lambda *refs: pack_kernel(mesh_rows, *refs),
        [shape((rows + 16, channels), bf16)],
        [],
        latent[0], neighbours, live, edge_weight,
    )
    received = shifted(message, "space", 1)
    moved = shifted(
        jnp.concatenate([targets[:, half:], area[None, half:]], axis=0), "space", 1
    )
    copies, field, gate, adjacency = call(
        lambda *refs: forward_kernel(mesh_rows, *refs),
        [
            shape((members, fields, points), bf16),
            shape((fields, points), f32),
            shape((channels, points), f32),
            shape((span, points), bf16),
        ],
        [pltpu.VMEM((2 * span, channels), bf16), pltpu.VMEM((channels, points), bf16)],
        received, latent[0], neighbours, live, edge_weight, w_in, w_out,
    )
    every = lax.all_to_all(copies, "member", 0, 0, tiled=True)
    inner, rim = call(
        backward_kernel,
        [shape((rows, channels), f32), shape((rows, channels), bf16)],
        [pltpu.VMEM((span, channels), bf16)],
        every, field, targets, area[None], moved, gate, adjacency, w_out, w_in,
    )
    after = shifted(rim, "space", -1)
    return (inner + after.astype(f32)).astype(bf16)[None]


def solution(mesh):
    return jax.shard_map(
        per_device,
        mesh=mesh,
        in_specs=(
            P("member", "space", None),
            P(None, "space"),
            P(None, "space"),
            P(None, "space"),
            P("space"),
            P(None, "space"),
            P(),
            P(),
        ),
        out_specs=P("member", "space", None),
        check_vma=False,
    )
```

```python
import jax
import jax.numpy as jnp
from jax import lax
from jax.experimental import pallas as pl
from jax.experimental.pallas import tpu as pltpu
from jax.sharding import PartitionSpec as P

smooth = 0.0025
bf16 = jnp.bfloat16
f32 = jnp.float32
STEP = 256
LIMITS = (48, 48, 48)
KEPT = 16640


def shifted(block, axis, by):
    size = lax.axis_size(axis)
    return lax.ppermute(block, axis, [(i, (i + by) % size) for i in range(size)])


def slope(diff):
    return diff * lax.rsqrt(diff * diff + smooth)


def product(left, right, over):
    return lax.dot_general(left, right, (over, ((), ())), preferred_element_type=f32)


def adjacent(span, edges):
    slots, half = edges.shape[0] // 2, edges.shape[1]
    row = lax.broadcasted_iota(jnp.int32, (span, half), 0)
    total = jnp.zeros((span, half), f32)
    for k in range(slots):
        place = edges[k : k + 1].astype(jnp.int32)
        total = total + jnp.where(row == place, edges[slots + k : slots + k + 1], 0.0)
    return total.astype(bf16)


def halves(part):
    top = part.astype(bf16)
    return top, (part - top.astype(f32)).astype(bf16)


def own_kernel(message, w_in, own_top, own_rest, own_edges):
    rows, channels = own_top.shape
    span, half = own_edges.shape
    tail = message[rows:, :half].astype(f32)
    own_edges[...] = adjacent(span, tail[tail.shape[0] // 2 :])
    for c in range(0, channels, STEP):
        cut = slice(c, c + STEP)
        part = product(message[:rows], w_in[:, cut], ((1,), (0,)))
        own_top[:, cut], own_rest[:, cut] = halves(part)


def forward_kernel(
    message, own_top, own_rest, own_edges, w_in, w_out, copies, kept,
    mixed, hidden, rounded, gates, edges, wide, done,
):
    rows, channels = own_top.shape
    span, half = own_edges.shape
    members, count, points = copies.shape
    sent = []

    def send(source, target):
        copy = pltpu.make_async_copy(source, target, done.at[len(sent)])
        copy.start()
        sent.append(copy)

    tail = message[rows:, :half].astype(f32)
    edges[:, :half] = adjacent(span, tail[: tail.shape[0] // 2])
    edges[:, half:] = own_edges[...]
    send(edges, kept.at[pl.ds(channels, span)])
    both = edges[...]
    twice = jnp.concatenate([both, both], axis=0)
    for c in range(0, channels, STEP):
        cut = slice(c, c + STEP)
        part = product(message[:rows], w_in[:, cut], ((1,), (0,)))
        mixed[:rows, cut], mixed[span : span + rows, cut] = halves(part)
    mixed[rows:span] = own_top[...]
    mixed[span + rows :] = own_rest[...]
    for c in range(0, channels, STEP):
        cut = slice(c, c + STEP)
        pre = product(mixed[:, cut], twice, ((0,), (0,)))
        sigma = 1.0 / (1.0 + jnp.exp(-pre))
        act = pre * sigma
        hidden[cut] = act.astype(bf16)
        gates[cut] = (sigma + act * (1.0 - sigma)).astype(bf16)
        send(gates.at[pl.ds(c, STEP)], kept.at[pl.ds(c, STEP)])
    out = product(w_out[...], hidden[...], ((1,), (0,)))
    rounded[...] = out.astype(bf16)
    for m in range(members):
        send(rounded, copies.at[m])
    room = wide.shape[0] // 2
    padded = jnp.concatenate([out, jnp.zeros((room - count, points), f32)], axis=0)
    wide[:room], wide[room:] = halves(padded)
    send(wide, kept.at[pl.ds(channels + span, 2 * room)])
    for copy in sent:
        copy.wait()


def backward_kernel(
    every, moved, targets, area, w_out, w_in, kept, out, rim,
    joined, gates, edges, wide, done,
):
    members, count, points = every.shape
    half = points // 2
    rows, channels = out.shape
    span = 2 * rows
    room = wide.shape[0] // 2
    loads = [(kept.at[pl.ds(channels + span, 2 * room)], wide)]
    loads += [(kept.at[pl.ds(c, STEP)], gates.at[pl.ds(c, STEP)]) for c in range(0, channels, STEP)]
    loads += [(kept.at[pl.ds(channels, span)], edges)]
    loads = [pltpu.make_async_copy(*pair, done.at[i]) for i, pair in enumerate(loads)]
    for copy in loads:
        copy.start()
    me = lax.axis_index("member")
    loads[0].wait()
    own = (wide[:room].astype(f32) + wide[room:].astype(f32))[:count]
    total = jnp.zeros((count, points), f32)
    for m in range(members):
        total = total + slope(own - every[m].astype(f32)) * jnp.where(me == m, 0.0, 1.0 / (members - 1))
    goal = jnp.concatenate([moved[:count], targets[:, :half]], axis=1)
    scale = jnp.concatenate([moved[count : count + 1], area[:, :half]], axis=1)
    grad_field = (scale * (slope(own - goal) - total)).astype(bf16)
    for copy in loads[1:]:
        copy.wait()
    for c in range(0, channels, STEP):
        cut = slice(c, c + STEP)
        grad_hidden = product(w_out[:, cut], grad_field, ((0,), (0,)))
        grad_pre = (grad_hidden * gates[cut].astype(f32)).astype(bf16)
        joined[:, cut] = product(edges[...], grad_pre, ((1,), (1,))).astype(bf16)
    for c in range(0, channels, STEP):
        cut = slice(c, c + STEP)
        part = product(joined[...], w_in[cut], ((1,), (1,)))
        rim[:, cut] = part[:rows].astype(bf16)
        out[:, cut] = part[rows:]


HERE = pl.BlockSpec(memory_space=pltpu.VMEM)
AWAY = pl.BlockSpec(memory_space=pl.ANY)


def call(kernel, limit, ins, outs, scratch, copies=0):
    return pl.pallas_call(
        kernel,
        out_shape=[jax.ShapeDtypeStruct(dims, kind) for _, dims, kind in outs],
        in_specs=[spec for spec, _ in ins],
        out_specs=[spec for spec, _, _ in outs],
        scratch_shapes=[pltpu.VMEM(dims, kind) for dims, kind in scratch]
        + [pltpu.SemaphoreType.DMA((copies,))] * (copies > 0),
        compiler_params=pltpu.CompilerParams(vmem_limit_bytes=limit << 20),
        cost_estimate=pl.CostEstimate(flops=10**10, bytes_accessed=4 << 20, transcendentals=0),
    )(*[operand for _, operand in ins])


def per_device(latent, neighbours, live, edge_weight, area, targets, w_in, w_out):
    rows, channels = latent.shape[1:]
    slots, points = neighbours.shape
    fields = targets.shape[0]
    half = points // 2
    mesh_rows = rows * lax.axis_size("space")
    members = lax.axis_size("member")
    span = 2 * rows
    room = -(-fields // 16) * 16

    first = lax.axis_index("space") * rows
    coef = edge_weight * live.astype(bf16)
    high = jnp.bitwise_and(neighbours[:, half:] - first, mesh_rows - 1).astype(bf16)
    low = jnp.bitwise_and(neighbours[:, :half] - (first - rows), mesh_rows - 1).astype(bf16)
    tail = jnp.concatenate([high, coef[:, half:], low, coef[:, :half]], axis=0)
    message = jnp.concatenate([latent[0], jnp.pad(tail, ((0, 0), (0, channels - half)))], axis=0)
    received = shifted(message, "space", 1)
    own_top, own_rest, own_edges = call(
        own_kernel,
        LIMITS[0],
        [(HERE, message), (HERE, w_in)],
        [(HERE, (rows, channels), bf16), (HERE, (rows, channels), bf16), (HERE, (span, half), bf16)],
        [],
    )
    moved = shifted(
        jnp.concatenate([targets[:, half:], area[None, half:]], axis=0), "space", 1
    )
    copies, kept = call(
        forward_kernel,
        LIMITS[1],
        [(HERE, x) for x in (received, own_top, own_rest, own_edges, w_in, w_out)],
        [
            (AWAY, (members, fields, points), bf16),
            (AWAY, (KEPT, points), bf16),
        ],
        [
            ((2 * span, channels), bf16),
            ((channels, points), bf16),
            ((fields, points), bf16),
            ((channels, points), bf16),
            ((span, points), bf16),
            ((2 * room, points), bf16),
        ],
        members + channels // STEP + 2,
    )
    every = lax.all_to_all(copies, "member", 0, 0, tiled=True)
    inner, rim = call(
        backward_kernel,
        LIMITS[2],
        [(HERE, x) for x in (every, moved, targets, area[None], w_out, w_in)] + [(AWAY, kept)],
        [(HERE, (rows, channels), f32), (HERE, (rows, channels), bf16)],
        [
            ((span, channels), bf16),
            ((channels, points), bf16),
            ((span, points), bf16),
            ((2 * room, points), bf16),
        ],
        channels // STEP + 2,
    )
    after = shifted(rim, "space", -1)
    return (inner + after.astype(f32)).astype(bf16)[None]


def solution(mesh):
    return jax.shard_map(
        per_device,
        mesh=mesh,
        in_specs=(
            P("member", "space", None),
            P(None, "space"),
            P(None, "space"),
            P(None, "space"),
            P("space"),
            P(None, "space"),
            P(),
            P(),
        ),
        out_specs=P("member", "space", None),
        check_vma=False,
    )
```

```python
import jax
import jax.numpy as jnp
from jax import lax
from jax.experimental import pallas as pl
from jax.experimental.pallas import tpu as pltpu
from jax.sharding import PartitionSpec as P

smooth = 0.0025
bf16 = jnp.bfloat16
f32 = jnp.float32
STEP = 256
LIMITS = (16, 16, 16)
SLOTS = 4


def shifted(block, axis, by):
    size = lax.axis_size(axis)
    return lax.ppermute(block, axis, [(i, (i + by) % size) for i in range(size)])


def slope(diff):
    return diff * lax.rsqrt(diff * diff + smooth)


def product(left, right, over):
    return lax.dot_general(left, right, (over, ((), ())), preferred_element_type=f32)


def adjacent(span, edges):
    slots, half = SLOTS, edges.shape[1]
    row = lax.broadcasted_iota(jnp.int32, (span, half), 0)
    total = jnp.zeros((span, half), f32)
    for k in range(slots):
        place = edges[k : k + 1].astype(jnp.int32)
        total = total + jnp.where(row == place, edges[slots + k : slots + k + 1], 0.0)
    return total.astype(bf16)


def halves(part):
    top = part.astype(bf16)
    return top, (part - top.astype(f32)).astype(bf16)


def pack_kernel(latent, place, coef, message):
    rows, (slots, points) = latent.shape[0], place.shape
    message[:rows] = latent[...]
    blank = jnp.zeros((16 - 2 * slots, points), f32)
    tail = jnp.concatenate([place[...], coef[...], blank], axis=0)
    message[rows:, :points] = tail.astype(bf16)
    message[rows:, points:] = jnp.zeros((16, message.shape[1] - points), bf16)


def goal_kernel(targets, area, message):
    count, half = targets.shape[0], message.shape[1]
    message[:count] = targets[:, half:]
    message[count : count + 1] = area[:, half:]


def own_kernel(message, w_in, own_top, own_rest, own_edges):
    rows, channels = own_top.shape
    span, half = own_edges.shape
    own_edges[...] = adjacent(span, message[rows:, :half].astype(f32))
    for c in range(0, channels, STEP):
        cut = slice(c, c + STEP)
        part = product(message[:rows], w_in[:, cut], ((1,), (0,)))
        own_top[:, cut], own_rest[:, cut] = halves(part)


def forward_kernel(
    message, own_top, own_rest, own_edges, w_in, w_out, copies, field, gate, edges, mixed, hidden
):
    rows, channels = own_top.shape
    span, half = own_edges.shape
    edges[:, :half] = adjacent(span, message[rows:, half : 2 * half].astype(f32))
    edges[:, half:] = own_edges[...]
    both = edges[...]
    twice = jnp.concatenate([both, both], axis=0)
    for c in range(0, channels, STEP):
        cut = slice(c, c + STEP)
        part = product(message[:rows], w_in[:, cut], ((1,), (0,)))
        mixed[:rows, cut], mixed[span : span + rows, cut] = halves(part)
    mixed[rows:span] = own_top[...]
    mixed[span + rows :] = own_rest[...]
    for c in range(0, channels, STEP):
        cut = slice(c, c + STEP)
        pre = product(mixed[:, cut], twice, ((0,), (0,)))
        sigma = 1.0 / (1.0 + jnp.exp(-pre))
        act = pre * sigma
        hidden[cut] = act.astype(bf16)
        gate[cut] = sigma + act * (1.0 - sigma)
    out = product(w_out[...], hidden[...], ((1,), (0,)))
    field[...] = out
    rounded = out.astype(bf16)
    for m in range(copies.shape[0]):
        copies[m] = rounded


def backward_kernel(
    every, moved, targets, area, w_out, w_in, field, gate, edges, out, rim, joined
):
    members, count, points = every.shape
    half = points // 2
    rows, channels = out.shape
    me = lax.axis_index("member")
    own = every[me].astype(f32)
    total = jnp.zeros((count, points), f32)
    for m in range(members):
        total = total + slope(own - every[m].astype(f32))
    goal = jnp.concatenate([moved[:count], targets[:, :half]], axis=1)
    scale = jnp.concatenate([moved[count : count + 1], area[:, :half]], axis=1)
    pull = slope(field[...] - goal) - total * (1.0 / (members - 1))
    grad_field = (scale * pull).astype(bf16)
    for c in range(0, channels, STEP):
        cut = slice(c, c + STEP)
        grad_hidden = product(w_out[:, cut], grad_field, ((0,), (0,)))
        grad_pre = (grad_hidden * gate[cut]).astype(bf16)
        joined[:, cut] = product(edges[...], grad_pre, ((1,), (1,))).astype(bf16)
    for c in range(0, channels, STEP):
        cut = slice(c, c + STEP)
        part = product(joined[...], w_in[cut], ((1,), (1,)))
        rim[:, cut] = part[:rows].astype(bf16)
        out[:, cut] = part[rows:]


HERE = pl.BlockSpec(memory_space=pltpu.VMEM)


def call(kernel, limit, ins, outs, scratch):
    return pl.pallas_call(
        kernel,
        out_shape=[jax.ShapeDtypeStruct(dims, kind) for _, dims, kind in outs],
        in_specs=[spec for spec, _ in ins],
        out_specs=[spec for spec, _, _ in outs],
        scratch_shapes=[pltpu.VMEM(dims, kind) for dims, kind in scratch],
        compiler_params=pltpu.CompilerParams(vmem_limit_bytes=limit << 20),
        cost_estimate=pl.CostEstimate(flops=10**10, bytes_accessed=4 << 20, transcendentals=0),
    )(*[operand for _, operand in ins])


def per_device(latent, neighbours, live, edge_weight, area, targets, w_in, w_out):
    rows, channels = latent.shape[1:]
    slots, points = neighbours.shape
    fields = targets.shape[0]
    half = points // 2
    mesh_rows = rows * lax.axis_size("space")
    members = lax.axis_size("member")
    span = 2 * rows

    column = lax.broadcasted_iota(jnp.int32, (slots, points), 1)
    first = (lax.axis_index("space") - (column < half)) * rows
    place = jnp.bitwise_and(neighbours - first, mesh_rows - 1).astype(f32)
    coef = edge_weight.astype(f32) * live.astype(f32)
    edge = 4.0 * place + coef
    place = jnp.floor(0.25 * edge)
    coef = edge - 4.0 * place
    (message,) = call(
        pack_kernel,
        LIMITS[0],
        [(HERE, x) for x in (latent[0], place, coef)],
        [(HERE, (rows + 16, channels), bf16)],
        [],
    )
    received = shifted(message, "space", 1)
    own_top, own_rest, own_edges = call(
        own_kernel,
        LIMITS[0],
        [(HERE, message), (HERE, w_in)],
        [(HERE, (rows, channels), bf16), (HERE, (rows, channels), bf16), (HERE, (span, half), bf16)],
        [],
    )
    own_edges, targets, area = lax.optimization_barrier((own_edges, targets, area[None]))
    (goals,) = call(
        goal_kernel, LIMITS[0], [(HERE, targets), (HERE, area)], [(HERE, (fields + 4, half), f32)], []
    )
    moved = shifted(goals, "space", 1)
    copies, field, gate, edges = call(
        forward_kernel,
        LIMITS[1],
        [(HERE, x) for x in (received, own_top, own_rest, own_edges, w_in, w_out)],
        [
            (HERE, (members, fields, points), bf16),
            (HERE, (fields, points), f32),
            (HERE, (channels, points), f32),
            (HERE, (span, points), bf16),
        ],
        [((2 * span, channels), bf16), ((channels, points), bf16)],
    )
    copies, moved = lax.optimization_barrier((copies, moved))
    every = lax.all_to_all(copies, "member", 0, 0, tiled=True)
    inner, rim = call(
        backward_kernel,
        LIMITS[2],
        [(HERE, x) for x in (every, moved, targets, area, w_out, w_in, field, gate, edges)],
        [(HERE, (rows, channels), f32), (HERE, (rows, channels), bf16)],
        [((span, channels), bf16)],
    )
    after = shifted(rim, "space", -1)
    return (inner + after.astype(f32)).astype(bf16)[None]


def solution(mesh):
    return jax.shard_map(
        per_device,
        mesh=mesh,
        in_specs=(
            P("member", "space", None),
            P(None, "space"),
            P(None, "space"),
            P(None, "space"),
            P("space"),
            P(None, "space"),
            P(),
            P(),
        ),
        out_specs=P("member", "space", None),
        check_vma=False,
    )
```

```python
import jax
import jax.numpy as jnp
from jax import lax
from jax.experimental import pallas as pl
from jax.experimental.pallas import tpu as pltpu
from jax.sharding import PartitionSpec as P

smooth = 0.0025
bf16 = jnp.bfloat16
f32 = jnp.float32
STEP = 256
LIMITS = (16, 16, 16)
SLOTS = 4


def shifted(block, axis, by):
    size = lax.axis_size(axis)
    return lax.ppermute(block, axis, [(i, (i + by) % size) for i in range(size)])


def slope(diff):
    return diff * lax.rsqrt(diff * diff + smooth)


def product(left, right, over):
    return lax.dot_general(left, right, (over, ((), ())), preferred_element_type=f32)


def adjacent(span, edges):
    slots, half = SLOTS, edges.shape[1]
    row = lax.broadcasted_iota(jnp.int32, (span, half), 0)
    total = jnp.zeros((span, half), f32)
    for k in range(slots):
        place = edges[k : k + 1].astype(jnp.int32)
        total = total + jnp.where(row == place, edges[slots + k : slots + k + 1], 0.0)
    return total.astype(bf16)


def halves(part):
    top = part.astype(bf16)
    return top, (part - top.astype(f32)).astype(bf16)


def goal_kernel(targets, area, message):
    count, half = targets.shape[0], message.shape[1]
    message[:count] = targets[:, half:]
    message[count : count + 1] = area[:, half:]


def edge_kernel(message, own_edges):
    span, half = own_edges.shape
    own_edges[...] = adjacent(span, message[span // 2 :, :half].astype(f32))


def own_kernel(message, w_in, own_top, own_rest):
    rows, channels = own_top.shape
    for c in range(0, channels, STEP):
        cut = slice(c, c + STEP)
        part = product(message[:rows], w_in[:, cut], ((1,), (0,)))
        own_top[:, cut], own_rest[:, cut] = halves(part)


def forward_kernel(
    message, own_top, own_rest, own_edges, w_in, w_out, copies, field, gate, edges, mixed, hidden
):
    rows, channels = own_top.shape
    span, half = own_edges.shape
    edges[:, :half] = adjacent(span, message[rows:, half : 2 * half].astype(f32))
    edges[:, half:] = own_edges[...]
    both = edges[...]
    twice = jnp.concatenate([both, both], axis=0)
    for c in range(0, channels, STEP):
        cut = slice(c, c + STEP)
        part = product(message[:rows], w_in[:, cut], ((1,), (0,)))
        mixed[:rows, cut], mixed[span : span + rows, cut] = halves(part)
    mixed[rows:span] = own_top[...]
    mixed[span + rows :] = own_rest[...]
    for c in range(0, channels, STEP):
        cut = slice(c, c + STEP)
        pre = product(mixed[:, cut], twice, ((0,), (0,)))
        sigma = 1.0 / (1.0 + jnp.exp(-pre))
        act = pre * sigma
        hidden[cut] = act.astype(bf16)
        gate[cut] = sigma + act * (1.0 - sigma)
    out = product(w_out[...], hidden[...], ((1,), (0,)))
    field[...] = out
    rounded = out.astype(bf16)
    for m in range(copies.shape[0]):
        copies[m] = rounded


def backward_kernel(
    every, moved, targets, area, w_out, w_in, field, gate, edges, out, rim, joined
):
    members, count, points = every.shape
    half = points // 2
    rows, channels = out.shape
    me = lax.axis_index("member")
    own = every[me].astype(f32)
    total = jnp.zeros((count, points), f32)
    for m in range(members):
        total = total + slope(own - every[m].astype(f32))
    goal = jnp.concatenate([moved[:count], targets[:, :half]], axis=1)
    scale = jnp.concatenate([moved[count : count + 1], area[:, :half]], axis=1)
    pull = slope(field[...] - goal) - total * (1.0 / (members - 1))
    grad_field = (scale * pull).astype(bf16)
    for c in range(0, channels, STEP):
        cut = slice(c, c + STEP)
        grad_hidden = product(w_out[:, cut], grad_field, ((0,), (0,)))
        grad_pre = (grad_hidden * gate[cut]).astype(bf16)
        joined[:, cut] = product(edges[...], grad_pre, ((1,), (1,))).astype(bf16)
    for c in range(0, channels, STEP):
        cut = slice(c, c + STEP)
        part = product(joined[...], w_in[cut], ((1,), (1,)))
        rim[:, cut] = part[:rows].astype(bf16)
        out[:, cut] = part[rows:]


HERE = pl.BlockSpec(memory_space=pltpu.VMEM)


def call(kernel, limit, ins, outs, scratch):
    return pl.pallas_call(
        kernel,
        out_shape=[jax.ShapeDtypeStruct(dims, kind) for _, dims, kind in outs],
        in_specs=[spec for spec, _ in ins],
        out_specs=[spec for spec, _, _ in outs],
        scratch_shapes=[pltpu.VMEM(dims, kind) for dims, kind in scratch],
        compiler_params=pltpu.CompilerParams(vmem_limit_bytes=limit << 20),
        cost_estimate=pl.CostEstimate(flops=10**10, bytes_accessed=4 << 20, transcendentals=0),
    )(*[operand for _, operand in ins])


def per_device(latent, neighbours, live, edge_weight, area, targets, w_in, w_out):
    rows, channels = latent.shape[1:]
    slots, points = neighbours.shape
    fields = targets.shape[0]
    half = points // 2
    mesh_rows = rows * lax.axis_size("space")
    members = lax.axis_size("member")
    span = 2 * rows

    tall, blank = rows + 16, channels - points
    row = lax.broadcasted_iota(jnp.int32, (tall, channels), 0)
    column = lax.broadcasted_iota(jnp.int32, (tall, channels), 1)

    def placed(block, start):
        return jnp.pad(block, ((start, tall - start - block.shape[0]), (0, channels - block.shape[1])))

    first = (lax.axis_index("space") - (column < half)) * rows
    place = jnp.bitwise_and(placed(neighbours, rows) - first, mesh_rows - 1).astype(bf16)
    coef = placed(edge_weight, rows + slots).astype(f32) * placed(live, rows + slots).astype(f32)
    edge = jnp.where(row < rows + slots, place, coef.astype(bf16))
    message = jnp.where(row < rows, placed(latent[0], 0), edge)
    received = shifted(message, "space", 1)
    (own_edges,) = call(edge_kernel, LIMITS[0], [(HERE, message)], [(HERE, (span, half), bf16)], [])
    own_edges, targets, area = lax.optimization_barrier((own_edges, targets, area[None]))
    (goals,) = call(
        goal_kernel, LIMITS[0], [(HERE, targets), (HERE, area)], [(HERE, (fields + 4, half), f32)], []
    )
    moved = shifted(goals, "space", 1)
    own_top, own_rest = call(
        own_kernel,
        LIMITS[0],
        [(HERE, message), (HERE, w_in)],
        [(HERE, (rows, channels), bf16), (HERE, (rows, channels), bf16)],
        [],
    )
    copies, field, gate, edges = call(
        forward_kernel,
        LIMITS[1],
        [(HERE, x) for x in (received, own_top, own_rest, own_edges, w_in, w_out)],
        [
            (HERE, (members, fields, points), bf16),
            (HERE, (fields, points), f32),
            (HERE, (channels, points), f32),
            (HERE, (span, points), bf16),
        ],
        [((2 * span, channels), bf16), ((channels, points), bf16)],
    )
    copies, moved = lax.optimization_barrier((copies, moved))
    every = lax.all_to_all(copies, "member", 0, 0, tiled=True)
    inner, rim = call(
        backward_kernel,
        LIMITS[2],
        [(HERE, x) for x in (every, moved, targets, area, w_out, w_in, field, gate, edges)],
        [(HERE, (rows, channels), f32), (HERE, (rows, channels), bf16)],
        [((span, channels), bf16)],
    )
    after = shifted(rim, "space", -1)
    return (inner + after.astype(f32)).astype(bf16)[None]


def solution(mesh):
    return jax.shard_map(
        per_device,
        mesh=mesh,
        in_specs=(
            P("member", "space", None),
            P(None, "space"),
            P(None, "space"),
            P(None, "space"),
            P("space"),
            P(None, "space"),
            P(),
            P(),
        ),
        out_specs=P("member", "space", None),
        check_vma=False,
    )
```

```python
import jax
import jax.numpy as jnp
from jax import lax
from jax.experimental import pallas as pl
from jax.experimental.pallas import tpu as pltpu
from jax.sharding import PartitionSpec as P

smooth = 0.0025
bf16 = jnp.bfloat16
f32 = jnp.float32
STEP = 256
LANES = 128
LIMITS = (16, 16, 16)
SLOTS = 4


def shifted(block, axis, by):
    size = lax.axis_size(axis)
    return lax.ppermute(block, axis, [(i, (i + by) % size) for i in range(size)])


def slope(diff):
    return diff * lax.rsqrt(diff * diff + smooth)


def product(left, right, over):
    return lax.dot_general(left, right, (over, ((), ())), preferred_element_type=f32)


def adjacent(span, edges):
    slots, half = SLOTS, edges.shape[1]
    row = lax.broadcasted_iota(jnp.int32, (span, half), 0)
    total = jnp.zeros((span, half), f32)
    for k in range(slots):
        place = edges[k : k + 1].astype(jnp.int32)
        total = total + jnp.where(row == place, edges[slots + k : slots + k + 1], 0.0)
    return total.astype(bf16)


def halves(part):
    top = part.astype(bf16)
    return top, (part - top.astype(f32)).astype(bf16)


def goal_kernel(targets, area, message):
    count, half = targets.shape[0], message.shape[1]
    message[:count] = targets[:, half:]
    message[count : count + 1] = area[:, half:]


def packed(block):
    count, points = block.shape
    whole = count // 16 * 16
    cuts = [slice(j, j + LANES) for j in range(0, points, LANES)]
    return jnp.concatenate([block[:whole, cut] for cut in cuts] + [block[whole:, cut] for cut in cuts], axis=0)


def unpacked(block, count):
    parts = block.shape[0] // count
    whole = count // 16 * 16
    left, base = count - whole, parts * whole
    high = [block[j * whole : (j + 1) * whole] for j in range(parts)]
    low = [block[base + j * left : base + (j + 1) * left] for j in range(parts)]
    return jnp.concatenate([jnp.concatenate(high, axis=1), jnp.concatenate(low, axis=1)], axis=0)


def edge_kernel(message, own_edges):
    span, half = own_edges.shape
    own_edges[...] = adjacent(span, message[span // 2 :, :half].astype(f32))


def own_kernel(message, w_in, own_top, own_rest, turned):
    rows, channels = own_top.shape
    for c in range(0, channels, STEP):
        cut = slice(c, c + STEP)
        part = product(message[:rows], w_in[:, cut], ((1,), (0,)))
        own_top[:, cut], own_rest[:, cut] = halves(part)
    for c in range(0, channels, STEP):
        cut = slice(c, c + STEP)
        turned[:, cut] = w_in[cut].T


def forward_kernel(
    message, own_top, own_rest, own_edges, w_in, w_out, copies, field, gate, edges, mixed, hidden
):
    rows, channels = own_top.shape
    span, half = own_edges.shape
    edges[:, :half] = adjacent(span, message[rows:, half : 2 * half].astype(f32))
    edges[:, half:] = own_edges[...]
    both = edges[...]
    twice = jnp.concatenate([both, both], axis=0)
    for c in range(0, channels, STEP):
        cut = slice(c, c + STEP)
        part = product(message[:rows], w_in[:, cut], ((1,), (0,)))
        mixed[:rows, cut], mixed[span : span + rows, cut] = halves(part)
    mixed[rows:span] = own_top[...]
    mixed[span + rows :] = own_rest[...]
    for c in range(0, channels, STEP):
        cut = slice(c, c + STEP)
        pre = product(mixed[:, cut], twice, ((0,), (0,)))
        sigma = 1.0 / (1.0 + jnp.exp(-pre))
        act = pre * sigma
        hidden[cut] = act.astype(bf16)
        gate[cut] = sigma + act * (1.0 - sigma)
    out = product(w_out[...], hidden[...], ((1,), (0,)))
    field[...] = out
    rounded = packed(out).astype(bf16)
    for m in range(copies.shape[0]):
        copies[m] = rounded


def backward_kernel(
    every, moved, targets, area, w_out, turned, field, gate, edges, out, rim, joined
):
    members = every.shape[0]
    count, points = field.shape
    half = points // 2
    rows, channels = out.shape
    me = lax.axis_index("member")
    own = every[me].astype(f32)
    total = jnp.zeros(own.shape, f32)
    for m in range(members):
        total = total + slope(own - every[m].astype(f32))
    total = unpacked(total, count)
    goal = jnp.concatenate([moved[:count], targets[:, :half]], axis=1)
    scale = jnp.concatenate([moved[count : count + 1], area[:, :half]], axis=1)
    pull = slope(field[...] - goal) - total * (1.0 / (members - 1))
    grad_field = (scale * pull).astype(bf16)
    for c in range(0, channels, STEP):
        cut = slice(c, c + STEP)
        grad_hidden = product(w_out[:, cut], grad_field, ((0,), (0,)))
        grad_pre = (grad_hidden * gate[cut]).astype(bf16)
        joined[:, cut] = product(edges[...], grad_pre, ((1,), (1,))).astype(bf16)
    for c in range(0, channels, STEP):
        cut = slice(c, c + STEP)
        part = product(joined[...], turned[:, cut], ((1,), (0,)))
        rim[:, cut] = part[:rows].astype(bf16)
        out[:, cut] = part[rows:]


HERE = pl.BlockSpec(memory_space=pltpu.VMEM)


def call(kernel, limit, ins, outs, scratch):
    return pl.pallas_call(
        kernel,
        out_shape=[jax.ShapeDtypeStruct(dims, kind) for _, dims, kind in outs],
        in_specs=[spec for spec, _ in ins],
        out_specs=[spec for spec, _, _ in outs],
        scratch_shapes=[pltpu.VMEM(dims, kind) for dims, kind in scratch],
        compiler_params=pltpu.CompilerParams(vmem_limit_bytes=limit << 20),
        cost_estimate=pl.CostEstimate(flops=10**10, bytes_accessed=4 << 20, transcendentals=0),
    )(*[operand for _, operand in ins])


def per_device(latent, neighbours, live, edge_weight, area, targets, w_in, w_out):
    rows, channels = latent.shape[1:]
    slots, points = neighbours.shape
    fields = targets.shape[0]
    half = points // 2
    mesh_rows = rows * lax.axis_size("space")
    members = lax.axis_size("member")
    span = 2 * rows

    tall = rows + 8
    row = lax.broadcasted_iota(jnp.int32, (tall, channels), 0)
    column = lax.broadcasted_iota(jnp.int32, (tall, channels), 1)

    def placed(block, start):
        return jnp.pad(block, ((start, tall - start - block.shape[0]), (0, channels - block.shape[1])))

    first = (lax.axis_index("space") - (column < half)) * rows
    place = jnp.bitwise_and(placed(neighbours, rows) - first, mesh_rows - 1).astype(bf16)
    coef = placed(edge_weight, rows + slots).astype(f32) * placed(live, rows + slots).astype(f32)
    edge = jnp.where(row < rows + slots, place, coef.astype(bf16))
    message = jnp.where(row < rows, placed(latent[0], 0), edge)
    received = shifted(message, "space", 1)
    (own_edges,) = call(edge_kernel, LIMITS[0], [(HERE, message)], [(HERE, (span, half), bf16)], [])
    own_edges, targets, area = lax.optimization_barrier((own_edges, targets, area[None]))
    (goals,) = call(
        goal_kernel, LIMITS[0], [(HERE, targets), (HERE, area)], [(HERE, (fields + 4, half), f32)], []
    )
    moved = shifted(goals, "space", 1)
    own_top, own_rest, turned = call(
        own_kernel,
        LIMITS[0],
        [(HERE, message), (HERE, w_in)],
        [
            (HERE, (rows, channels), bf16),
            (HERE, (rows, channels), bf16),
            (HERE, (channels, channels), bf16),
        ],
        [],
    )
    copies, field, gate, edges = call(
        forward_kernel,
        LIMITS[1],
        [(HERE, x) for x in (received, own_top, own_rest, own_edges, w_in, w_out)],
        [
            (HERE, (members, fields * points // LANES, LANES), bf16),
            (HERE, (fields, points), f32),
            (HERE, (channels, points), f32),
            (HERE, (span, points), bf16),
        ],
        [((2 * span, channels), bf16), ((channels, points), bf16)],
    )
    copies, moved = lax.optimization_barrier((copies, moved))
    every = lax.all_to_all(copies, "member", 0, 0, tiled=True)
    inner, rim = call(
        backward_kernel,
        LIMITS[2],
        [(HERE, x) for x in (every, moved, targets, area, w_out, turned, field, gate, edges)],
        [(HERE, (rows, channels), f32), (HERE, (rows, channels), bf16)],
        [((span, channels), bf16)],
    )
    after = shifted(rim, "space", -1)
    return (inner + after.astype(f32)).astype(bf16)[None]


def solution(mesh):
    return jax.shard_map(
        per_device,
        mesh=mesh,
        in_specs=(
            P("member", "space", None),
            P(None, "space"),
            P(None, "space"),
            P(None, "space"),
            P("space"),
            P(None, "space"),
            P(),
            P(),
        ),
        out_specs=P("member", "space", None),
        check_vma=False,
    )
```

```python
import jax
import jax.numpy as jnp
from jax import lax
from jax.experimental import pallas as pl
from jax.experimental.pallas import tpu as pltpu
from jax.sharding import PartitionSpec as P

smooth = 0.0025
bf16 = jnp.bfloat16
f32 = jnp.float32
STEP = 256
LANES = 128
LIMITS = (16, 16, 16)
SLOTS = 4


def shifted(block, axis, by):
    size = lax.axis_size(axis)
    return lax.ppermute(block, axis, [(i, (i + by) % size) for i in range(size)])


def slope(diff):
    return diff * lax.rsqrt(diff * diff + smooth)


def product(left, right, over):
    return lax.dot_general(left, right, (over, ((), ())), preferred_element_type=f32)


def adjacent(span, edges):
    slots, half = SLOTS, edges.shape[1]
    row = lax.broadcasted_iota(jnp.int32, (span, half), 0)
    total = jnp.zeros((span, half), f32)
    for k in range(slots):
        place = edges[k : k + 1].astype(jnp.int32)
        total = total + jnp.where(row == place, edges[slots + k : slots + k + 1], 0.0)
    return total.astype(bf16)


def halves(part):
    top = part.astype(bf16)
    return top, (part - top.astype(f32)).astype(bf16)


def goal_kernel(targets, area, message):
    count, half = targets.shape[0], message.shape[1]
    message[:count] = targets[:, half:]
    message[count : count + 1] = area[:, half:]


def packed(block):
    count, points = block.shape
    whole = count // 16 * 16
    cuts = [slice(j, j + LANES) for j in range(0, points, LANES)]
    return jnp.concatenate([block[:whole, cut] for cut in cuts] + [block[whole:, cut] for cut in cuts], axis=0)


def unpacked(block, count):
    parts = block.shape[0] // count
    whole = count // 16 * 16
    left, base = count - whole, parts * whole
    high = [block[j * whole : (j + 1) * whole] for j in range(parts)]
    low = [block[base + j * left : base + (j + 1) * left] for j in range(parts)]
    return jnp.concatenate([jnp.concatenate(high, axis=1), jnp.concatenate(low, axis=1)], axis=0)


def edge_kernel(message, own_edges):
    span, half = own_edges.shape
    own_edges[...] = adjacent(span, message[span // 2 :, :half].astype(f32))


def own_kernel(message, w_in, own_top, own_rest, turned):
    rows, channels = own_top.shape
    for c in range(0, channels, STEP):
        cut = slice(c, c + STEP)
        part = product(message[:rows], w_in[:, cut], ((1,), (0,)))
        own_top[:, cut], own_rest[:, cut] = halves(part)
    for c in range(0, channels, STEP):
        cut = slice(c, c + STEP)
        turned[:, cut] = w_in[cut].T


def forward_kernel(
    message, own_top, own_rest, own_edges, w_in, w_out, copies, field, gate, edges, mixed, hidden
):
    rows, channels = own_top.shape
    span, half = own_edges.shape
    edges[:, :half] = adjacent(span, message[rows:, half : 2 * half].astype(f32))
    edges[:, half:] = own_edges[...]
    both = edges[...]
    twice = jnp.concatenate([both, both], axis=0)
    for c in range(0, channels, STEP):
        cut = slice(c, c + STEP)
        part = product(message[:rows], w_in[:, cut], ((1,), (0,)))
        mixed[:rows, cut], mixed[span : span + rows, cut] = halves(part)
    mixed[rows:span] = own_top[...]
    mixed[span + rows :] = own_rest[...]
    for c in range(0, channels, STEP):
        cut = slice(c, c + STEP)
        pre = product(mixed[:, cut], twice, ((0,), (0,)))
        sigma = 1.0 / (1.0 + jnp.exp(-pre))
        act = pre * sigma
        hidden[cut] = act.astype(bf16)
        gate[cut] = sigma + act * (1.0 - sigma)
    out = product(w_out[...], hidden[...], ((1,), (0,)))
    field[...] = out
    rounded = packed(out).astype(bf16)
    for m in range(copies.shape[0]):
        copies[m] = rounded


def backward_kernel(
    every, moved, targets, area, w_out, turned, field, gate, edges, out, rim, joined
):
    members = every.shape[0]
    count, points = field.shape
    half = points // 2
    rows, channels = out.shape
    me = lax.axis_index("member")
    own = every[me].astype(f32)
    total = jnp.zeros(own.shape, f32)
    for m in range(members):
        total = total + slope(own - every[m].astype(f32))
    total = unpacked(total, count)
    goal = jnp.concatenate([moved[:count], targets[:, :half]], axis=1)
    scale = jnp.concatenate([moved[count : count + 1], area[:, :half]], axis=1)
    pull = slope(field[...] - goal) - total * (1.0 / (members - 1))
    grad_field = (scale * pull).astype(bf16)
    for c in range(0, channels, STEP):
        cut = slice(c, c + STEP)
        grad_hidden = product(w_out[:, cut], grad_field, ((0,), (0,)))
        grad_pre = (grad_hidden * gate[cut]).astype(bf16)
        joined[:, cut] = product(edges[...], grad_pre, ((1,), (1,))).astype(bf16)
    for c in range(0, channels, STEP):
        cut = slice(c, c + STEP)
        part = product(joined[...], turned[:, cut], ((1,), (0,)))
        rim[:, cut] = part[:rows].astype(bf16)
        out[:, cut] = part[rows:]


HERE = pl.BlockSpec(memory_space=pltpu.VMEM)


def call(kernel, limit, ins, outs, scratch):
    return pl.pallas_call(
        kernel,
        out_shape=[jax.ShapeDtypeStruct(dims, kind) for _, dims, kind in outs],
        in_specs=[spec for spec, _ in ins],
        out_specs=[spec for spec, _, _ in outs],
        scratch_shapes=[pltpu.VMEM(dims, kind) for dims, kind in scratch],
        compiler_params=pltpu.CompilerParams(vmem_limit_bytes=limit << 20),
        cost_estimate=pl.CostEstimate(flops=10**10, bytes_accessed=4 << 20, transcendentals=0),
    )(*[operand for _, operand in ins])


def per_device(latent, neighbours, live, edge_weight, area, targets, w_in, w_out):
    rows, channels = latent.shape[1:]
    slots, points = neighbours.shape
    fields = targets.shape[0]
    half = points // 2
    mesh_rows = rows * lax.axis_size("space")
    members = lax.axis_size("member")
    span = 2 * rows

    tall = rows + 16
    row = lax.broadcasted_iota(jnp.int32, (tall, channels), 0)
    column = lax.broadcasted_iota(jnp.int32, (tall, channels), 1)

    def placed(block, start):
        return jnp.pad(block, ((start, tall - start - block.shape[0]), (0, channels - block.shape[1])))

    first = (lax.axis_index("space") - (column < half)) * rows
    place = jnp.bitwise_and(placed(neighbours, rows) - first, mesh_rows - 1).astype(bf16)
    coef = placed(edge_weight, rows + slots).astype(f32) * placed(live, rows + slots).astype(f32)
    edge = jnp.where(row < rows + slots, place, coef.astype(bf16))
    message = jnp.where(row < rows, placed(latent[0], 0), edge)
    received = shifted(message, "space", 1)
    (own_edges,) = call(edge_kernel, LIMITS[0], [(HERE, message)], [(HERE, (span, half), bf16)], [])
    own_edges, targets, area = lax.optimization_barrier((own_edges, targets, area[None]))
    (goals,) = call(
        goal_kernel, LIMITS[0], [(HERE, targets), (HERE, area)], [(HERE, (fields + 4, half), f32)], []
    )
    moved = shifted(goals, "space", 1)
    own_top, own_rest, turned = call(
        own_kernel,
        LIMITS[0],
        [(HERE, message), (HERE, w_in)],
        [
            (HERE, (rows, channels), bf16),
            (HERE, (rows, channels), bf16),
            (HERE, (channels, channels), bf16),
        ],
        [],
    )
    copies, field, gate, edges = call(
        forward_kernel,
        LIMITS[1],
        [(HERE, x) for x in (received, own_top, own_rest, own_edges, w_in, w_out)],
        [
            (HERE, (members, fields * points // LANES, LANES), bf16),
            (HERE, (fields, points), f32),
            (HERE, (channels, points), f32),
            (HERE, (span, points), bf16),
        ],
        [((2 * span, channels), bf16), ((channels, points), bf16)],
    )
    copies, moved = lax.optimization_barrier((copies, moved))
    every = lax.all_to_all(copies, "member", 0, 0, tiled=True)
    inner, rim = call(
        backward_kernel,
        LIMITS[2],
        [(HERE, x) for x in (every, moved, targets, area, w_out, turned, field, gate, edges)],
        [(HERE, (rows, channels), f32), (HERE, (rows, channels), bf16)],
        [((span, channels), bf16)],
    )
    after = shifted(rim, "space", -1)
    return (inner + after.astype(f32)).astype(bf16)[None]


def solution(mesh):
    return jax.shard_map(
        per_device,
        mesh=mesh,
        in_specs=(
            P("member", "space", None),
            P(None, "space"),
            P(None, "space"),
            P(None, "space"),
            P("space"),
            P(None, "space"),
            P(),
            P(),
        ),
        out_specs=P("member", "space", None),
        check_vma=False,
    )
```

```python
import jax
import jax.numpy as jnp
from jax import lax
from jax.experimental import pallas as pl
from jax.experimental.pallas import tpu as pltpu
from jax.sharding import PartitionSpec as P

smooth = 0.0025
bf16 = jnp.bfloat16
f32 = jnp.float32
STEP = 256
LANES = 128
LIMITS = (16, 16, 16)
SLOTS = 4


def shifted(block, axis, by):
    size = lax.axis_size(axis)
    return lax.ppermute(block, axis, [(i, (i + by) % size) for i in range(size)])


def slope(diff):
    return diff * lax.rsqrt(diff * diff + smooth)


def product(left, right, over):
    return lax.dot_general(left, right, (over, ((), ())), preferred_element_type=f32)


def adjacent(span, edges):
    slots, half = SLOTS, edges.shape[1]
    row = lax.broadcasted_iota(jnp.int32, (span, half), 0)
    total = jnp.zeros((span, half), f32)
    for k in range(slots):
        place = edges[k : k + 1].astype(jnp.int32)
        total = total + jnp.where(row == place, edges[slots + k : slots + k + 1], 0.0)
    return total.astype(bf16)


def goal_kernel(targets, area, message):
    count, half = targets.shape[0], message.shape[1]
    message[:count] = targets[:, half:]
    message[count : count + 1] = area[:, half:]


def packed(block):
    count, points = block.shape
    whole = count // 16 * 16
    cuts = [slice(j, j + LANES) for j in range(0, points, LANES)]
    return jnp.concatenate([block[:whole, cut] for cut in cuts] + [block[whole:, cut] for cut in cuts], axis=0)


def unpacked(block, count):
    parts = block.shape[0] // count
    whole = count // 16 * 16
    left, base = count - whole, parts * whole
    high = [block[j * whole : (j + 1) * whole] for j in range(parts)]
    low = [block[base + j * left : base + (j + 1) * left] for j in range(parts)]
    return jnp.concatenate([jnp.concatenate(high, axis=1), jnp.concatenate(low, axis=1)], axis=0)


def edge_kernel(message, own_edges):
    span, half = own_edges.shape
    own_edges[...] = adjacent(span, message[span // 2 :, :half].astype(f32))


def own_kernel(message, w_in, own_mixed, turned):
    rows, channels = own_mixed.shape
    for c in range(0, channels, STEP):
        cut = slice(c, c + STEP)
        own_mixed[:, cut] = product(message[:rows], w_in[:, cut], ((1,), (0,))).astype(bf16)
    for c in range(0, channels, STEP):
        cut = slice(c, c + STEP)
        turned[:, cut] = w_in[cut].T


def forward_kernel(
    message, own_mixed, own_edges, w_in, w_out, copies, field, gate, edges, mixed, hidden
):
    rows, channels = own_mixed.shape
    span, half = own_edges.shape
    edges[:, :half] = adjacent(span, message[rows:, half : 2 * half].astype(f32))
    edges[:, half:] = own_edges[...]
    for c in range(0, channels, STEP):
        cut = slice(c, c + STEP)
        mixed[:rows, cut] = product(message[:rows], w_in[:, cut], ((1,), (0,))).astype(bf16)
    mixed[rows:] = own_mixed[...]
    for c in range(0, channels, STEP):
        cut = slice(c, c + STEP)
        pre = product(mixed[:, cut], edges[...], ((0,), (0,)))
        sigma = 1.0 / (1.0 + jnp.exp(-pre))
        act = pre * sigma
        hidden[cut] = act.astype(bf16)
        gate[cut] = sigma + act * (1.0 - sigma)
    out = product(w_out[...], hidden[...], ((1,), (0,)))
    field[...] = out
    rounded = packed(out).astype(bf16)
    for m in range(copies.shape[0]):
        copies[m] = rounded


def backward_kernel(
    every, moved, targets, area, w_out, turned, field, gate, edges, out, rim, joined
):
    members = every.shape[0]
    count, points = field.shape
    half = points // 2
    rows, channels = out.shape
    me = lax.axis_index("member")
    own = every[me].astype(f32)
    total = jnp.zeros(own.shape, f32)
    for step in range(1, members):
        total = total + slope(own - every[lax.rem(me + step, members)].astype(f32))
    total = unpacked(total, count)
    goal = jnp.concatenate([moved[:count], targets[:, :half]], axis=1)
    scale = jnp.concatenate([moved[count : count + 1], area[:, :half]], axis=1)
    pull = slope(field[...] - goal) - total * (1.0 / (members - 1))
    grad_field = (scale * pull).astype(bf16)
    for c in range(0, channels, STEP):
        cut = slice(c, c + STEP)
        grad_hidden = product(w_out[:, cut], grad_field, ((0,), (0,)))
        grad_pre = (grad_hidden * gate[cut]).astype(bf16)
        joined[:, cut] = product(edges[...], grad_pre, ((1,), (1,))).astype(bf16)
    for c in range(0, channels, STEP):
        cut = slice(c, c + STEP)
        part = product(joined[...], turned[:, cut], ((1,), (0,)))
        rim[:, cut] = part[:rows].astype(bf16)
        out[:, cut] = part[rows:]


HERE = pl.BlockSpec(memory_space=pltpu.VMEM)


def call(kernel, limit, ins, outs, scratch):
    return pl.pallas_call(
        kernel,
        out_shape=[jax.ShapeDtypeStruct(dims, kind) for _, dims, kind in outs],
        in_specs=[spec for spec, _ in ins],
        out_specs=[spec for spec, _, _ in outs],
        scratch_shapes=[pltpu.VMEM(dims, kind) for dims, kind in scratch],
        compiler_params=pltpu.CompilerParams(vmem_limit_bytes=limit << 20),
        cost_estimate=pl.CostEstimate(flops=10**10, bytes_accessed=4 << 20, transcendentals=0),
    )(*[operand for _, operand in ins])


def per_device(latent, neighbours, live, edge_weight, area, targets, w_in, w_out):
    rows, channels = latent.shape[1:]
    slots, points = neighbours.shape
    fields = targets.shape[0]
    half = points // 2
    mesh_rows = rows * lax.axis_size("space")
    members = lax.axis_size("member")
    span = 2 * rows

    tall = rows + 16
    row = lax.broadcasted_iota(jnp.int32, (tall, channels), 0)
    column = lax.broadcasted_iota(jnp.int32, (tall, channels), 1)

    def placed(block, start):
        return jnp.pad(block, ((start, tall - start - block.shape[0]), (0, channels - block.shape[1])))

    first = (lax.axis_index("space") - (column < half)) * rows
    place = jnp.bitwise_and(placed(neighbours, rows) - first, mesh_rows - 1).astype(bf16)
    coef = placed(edge_weight, rows + slots).astype(f32) * placed(live, rows + slots).astype(f32)
    edge = jnp.where(row < rows + slots, place, coef.astype(bf16))
    message = jnp.where(row < rows, placed(latent[0], 0), edge)
    received = shifted(message, "space", 1)
    (own_edges,) = call(edge_kernel, LIMITS[0], [(HERE, message)], [(HERE, (span, half), bf16)], [])
    own_edges, targets, area = lax.optimization_barrier((own_edges, targets, area[None]))
    (goals,) = call(
        goal_kernel, LIMITS[0], [(HERE, targets), (HERE, area)], [(HERE, (fields + 4, half), f32)], []
    )
    moved = shifted(goals, "space", 1)
    own_mixed, turned = call(
        own_kernel,
        LIMITS[0],
        [(HERE, message), (HERE, w_in)],
        [(HERE, (rows, channels), bf16), (HERE, (channels, channels), bf16)],
        [],
    )
    copies, field, gate, edges = call(
        forward_kernel,
        LIMITS[1],
        [(HERE, x) for x in (received, own_mixed, own_edges, w_in, w_out)],
        [
            (HERE, (members, fields * points // LANES, LANES), bf16),
            (HERE, (fields, points), f32),
            (HERE, (channels, points), f32),
            (HERE, (span, points), bf16),
        ],
        [((span, channels), bf16), ((channels, points), bf16)],
    )
    copies, moved = lax.optimization_barrier((copies, moved))
    every = lax.all_to_all(copies, "member", 0, 0, tiled=True)
    inner, rim = call(
        backward_kernel,
        LIMITS[2],
        [(HERE, x) for x in (every, moved, targets, area, w_out, turned, field, gate, edges)],
        [(HERE, (rows, channels), f32), (HERE, (rows, channels), bf16)],
        [((span, channels), bf16)],
    )
    after = shifted(rim, "space", -1)
    return (inner + after.astype(f32)).astype(bf16)[None]


def solution(mesh):
    return jax.shard_map(
        per_device,
        mesh=mesh,
        in_specs=(
            P("member", "space", None),
            P(None, "space"),
            P(None, "space"),
            P(None, "space"),
            P("space"),
            P(None, "space"),
            P(),
            P(),
        ),
        out_specs=P("member", "space", None),
        check_vma=False,
    )
```

```python
import jax
import jax.numpy as jnp
from jax import lax
from jax.experimental import pallas as pl
from jax.experimental.pallas import tpu as pltpu
from jax.sharding import PartitionSpec as P

smooth = 0.0025
bf16 = jnp.bfloat16
f32 = jnp.float32
STEP = 256
LANES = 128
LIMITS = (16, 16, 16)
SLOTS = 4


def shifted(block, axis, by):
    size = lax.axis_size(axis)
    return lax.ppermute(block, axis, [(i, (i + by) % size) for i in range(size)])


def alternate(members):
    half = members // 2
    return [half * (i % 2) + i // 2 for i in range(members)]


def slope(diff):
    return diff * lax.rsqrt(diff * diff + smooth)


def product(left, right, over):
    return lax.dot_general(left, right, (over, ((), ())), preferred_element_type=f32)


def adjacent(span, edges):
    slots, half = SLOTS, edges.shape[1]
    row = lax.broadcasted_iota(jnp.int32, (span, half), 0)
    total = jnp.zeros((span, half), f32)
    for k in range(slots):
        place = edges[k : k + 1].astype(jnp.int32)
        total = total + jnp.where(row == place, edges[slots + k : slots + k + 1], 0.0)
    return total.astype(bf16)


def halves(part):
    top = part.astype(bf16)
    return top, (part - top.astype(f32)).astype(bf16)


def goal_kernel(targets, area, message):
    count, half = targets.shape[0], message.shape[1]
    message[:count] = targets[:, half:]
    message[count : count + 1] = area[:, half:]


def packed(block):
    count, points = block.shape
    whole = count // 16 * 16
    cuts = [slice(j, j + LANES) for j in range(0, points, LANES)]
    return jnp.concatenate([block[:whole, cut] for cut in cuts] + [block[whole:, cut] for cut in cuts], axis=0)


def unpacked(block, count):
    parts = block.shape[0] // count
    whole = count // 16 * 16
    left, base = count - whole, parts * whole
    high = [block[j * whole : (j + 1) * whole] for j in range(parts)]
    low = [block[base + j * left : base + (j + 1) * left] for j in range(parts)]
    return jnp.concatenate([jnp.concatenate(high, axis=1), jnp.concatenate(low, axis=1)], axis=0)


def edge_kernel(message, own_edges):
    span, half = own_edges.shape
    own_edges[...] = adjacent(span, message[span // 2 :, :half].astype(f32))


def own_kernel(message, w_in, own_top, own_rest, turned):
    rows, channels = own_top.shape
    for c in range(0, channels, STEP):
        cut = slice(c, c + STEP)
        part = product(message[:rows], w_in[:, cut], ((1,), (0,)))
        own_top[:, cut], own_rest[:, cut] = halves(part)
    for c in range(0, channels, STEP):
        cut = slice(c, c + STEP)
        turned[:, cut] = w_in[cut].T


def forward_kernel(
    message, own_top, own_rest, own_edges, w_in, w_out, copies, field, gate, edges, mixed, hidden
):
    rows, channels = own_top.shape
    span, half = own_edges.shape
    edges[:, :half] = adjacent(span, message[rows:, half : 2 * half].astype(f32))
    edges[:, half:] = own_edges[...]
    both = edges[...]
    twice = jnp.concatenate([both, both], axis=0)
    for c in range(0, channels, STEP):
        cut = slice(c, c + STEP)
        part = product(message[:rows], w_in[:, cut], ((1,), (0,)))
        mixed[:rows, cut], mixed[span : span + rows, cut] = halves(part)
    mixed[rows:span] = own_top[...]
    mixed[span + rows :] = own_rest[...]
    for c in range(0, channels, STEP):
        cut = slice(c, c + STEP)
        pre = product(mixed[:, cut], twice, ((0,), (0,)))
        sigma = 1.0 / (1.0 + jnp.exp(-pre))
        act = pre * sigma
        hidden[cut] = act.astype(bf16)
        gate[cut] = sigma + act * (1.0 - sigma)
    out = product(w_out[...], hidden[...], ((1,), (0,)))
    field[...] = out
    rounded = packed(out).astype(bf16)
    for m in range(copies.shape[0]):
        copies[m] = rounded


def backward_kernel(
    every, moved, targets, area, w_out, turned, field, gate, edges, out, rim, joined
):
    members = every.shape[0]
    count, points = field.shape
    half = points // 2
    rows, channels = out.shape
    half_row = members // 2
    member = lax.axis_index("member")
    me = 2 * lax.rem(member, half_row) + member // half_row
    own = every[me].astype(f32)
    total = jnp.zeros(own.shape, f32)
    for m in range(members):
        total = total + slope(own - every[m].astype(f32))
    total = unpacked(total, count)
    goal = jnp.concatenate([moved[:count], targets[:, :half]], axis=1)
    scale = jnp.concatenate([moved[count : count + 1], area[:, :half]], axis=1)
    pull = slope(field[...] - goal) - total * (1.0 / (members - 1))
    grad_field = (scale * pull).astype(bf16)
    for c in range(0, channels, STEP):
        cut = slice(c, c + STEP)
        grad_hidden = product(w_out[:, cut], grad_field, ((0,), (0,)))
        grad_pre = (grad_hidden * gate[cut]).astype(bf16)
        joined[:, cut] = product(edges[...], grad_pre, ((1,), (1,))).astype(bf16)
    for c in range(0, channels, STEP):
        cut = slice(c, c + STEP)
        part = product(joined[...], turned[:, cut], ((1,), (0,)))
        rim[:, cut] = part[:rows].astype(bf16)
        out[:, cut] = part[rows:]


HERE = pl.BlockSpec(memory_space=pltpu.VMEM)


def call(kernel, limit, ins, outs, scratch):
    return pl.pallas_call(
        kernel,
        out_shape=[jax.ShapeDtypeStruct(dims, kind) for _, dims, kind in outs],
        in_specs=[spec for spec, _ in ins],
        out_specs=[spec for spec, _, _ in outs],
        scratch_shapes=[pltpu.VMEM(dims, kind) for dims, kind in scratch],
        compiler_params=pltpu.CompilerParams(vmem_limit_bytes=limit << 20),
        cost_estimate=pl.CostEstimate(flops=10**10, bytes_accessed=4 << 20, transcendentals=0),
    )(*[operand for _, operand in ins])


def per_device(latent, neighbours, live, edge_weight, area, targets, w_in, w_out):
    rows, channels = latent.shape[1:]
    slots, points = neighbours.shape
    fields = targets.shape[0]
    half = points // 2
    mesh_rows = rows * lax.axis_size("space")
    members = lax.axis_size("member")
    span = 2 * rows

    tall = rows + 16
    row = lax.broadcasted_iota(jnp.int32, (tall, channels), 0)
    column = lax.broadcasted_iota(jnp.int32, (tall, channels), 1)

    def placed(block, start):
        return jnp.pad(block, ((start, tall - start - block.shape[0]), (0, channels - block.shape[1])))

    first = (lax.axis_index("space") - (column < half)) * rows
    place = jnp.bitwise_and(placed(neighbours, rows) - first, mesh_rows - 1).astype(bf16)
    coef = placed(edge_weight, rows + slots).astype(f32) * placed(live, rows + slots).astype(f32)
    edge = jnp.where(row < rows + slots, place, coef.astype(bf16))
    message = jnp.where(row < rows, placed(latent[0], 0), edge)
    received = shifted(message, "space", 1)
    (own_edges,) = call(edge_kernel, LIMITS[0], [(HERE, message)], [(HERE, (span, half), bf16)], [])
    own_edges, targets, area = lax.optimization_barrier((own_edges, targets, area[None]))
    (goals,) = call(
        goal_kernel, LIMITS[0], [(HERE, targets), (HERE, area)], [(HERE, (fields + 4, half), f32)], []
    )
    moved = shifted(goals, "space", 1)
    own_top, own_rest, turned = call(
        own_kernel,
        LIMITS[0],
        [(HERE, message), (HERE, w_in)],
        [
            (HERE, (rows, channels), bf16),
            (HERE, (rows, channels), bf16),
            (HERE, (channels, channels), bf16),
        ],
        [],
    )
    copies, field, gate, edges = call(
        forward_kernel,
        LIMITS[1],
        [(HERE, x) for x in (received, own_top, own_rest, own_edges, w_in, w_out)],
        [
            (HERE, (members, fields * points // LANES, LANES), bf16),
            (HERE, (fields, points), f32),
            (HERE, (channels, points), f32),
            (HERE, (span, points), bf16),
        ],
        [((2 * span, channels), bf16), ((channels, points), bf16)],
    )
    copies, moved = lax.optimization_barrier((copies, moved))
    every = lax.all_to_all(copies, "member", 0, 0, tiled=True, axis_index_groups=[alternate(members)])
    inner, rim = call(
        backward_kernel,
        LIMITS[2],
        [(HERE, x) for x in (every, moved, targets, area, w_out, turned, field, gate, edges)],
        [(HERE, (rows, channels), f32), (HERE, (rows, channels), bf16)],
        [((span, channels), bf16)],
    )
    after = shifted(rim, "space", -1)
    return (inner + after.astype(f32)).astype(bf16)[None]


def solution(mesh):
    return jax.shard_map(
        per_device,
        mesh=mesh,
        in_specs=(
            P("member", "space", None),
            P(None, "space"),
            P(None, "space"),
            P(None, "space"),
            P("space"),
            P(None, "space"),
            P(),
            P(),
        ),
        out_specs=P("member", "space", None),
        check_vma=False,
    )
```
